1024 devices in a mesh: ctx: 64 (over y, z_hi, x), dp: 16 (over z_lo, core).
Axes of the slice: x: 4, y: 8, z: 16 (z_hi: 2, z_lo: 8; z = z_hi * 8 + z_lo), core: 2. Of those that a mesh axis runs over, the one named last changes fastest.
Arguments:
- query: bfloat16 [16, 8192, 512], P('dp', 'ctx'), may hold values from -20 to 20
- key: bfloat16 [16, 8192, 512], P('dp', 'ctx'), may hold values from -20 to 20
- value: bfloat16 [16, 8192, 512], P('dp', 'ctx'), may hold values from -6 to 6
- table: int32 [128, 4], P('ctx'), may hold values from 0 to 127, as said below
- out_weight: bfloat16 [512, 512], replicated, may hold values from -0.25 to 0.25
- cotangent: bfloat16 [16, 8192, 512], P('dp', 'ctx'), may hold values from -6 to 6
Outputs:
- layer_out: bfloat16 [16, 8192, 512], P('dp', 'ctx')
- grad_query: bfloat16 [16, 8192, 512], P('dp', 'ctx')
- grad_key: bfloat16 [16, 8192, 512], P('dp', 'ctx')
- grad_value: bfloat16 [16, 8192, 512], P('dp', 'ctx')
- grad_weight: float32 [512, 512], replicated
The draws below stay inside these ranges and needn't reach their ends.
Inputs may be any that keep to these rules, and one draw needn't show every extreme that they name: `table`: row b names block b first; its other three ids are distinct, differ from b, and name blocks held on the same index of ctx as b or on the index just before or just after it, cyclically, where index c holds blocks c * 2 to (c + 1) * 2 - 1.
All inputs are finite; a program needn't handle non-finite values.
Results may differ from the reference program's by a relative error of at most 0.0086.
Values may be sent and summed in bfloat16 or wider, within the bound.
A program may use at most 32 MiB of HBM per device.

```python
import math
import jax
import jax.numpy as jnp
from jax import lax

D = 512
H = 8
BS = 64
BLK_DEV = 2
TOK_DEV = 128
NBLK = 128
TOKENS = 8192
SAMPLES = 16
N_CTX = 64


def draw_query(key, part):
    key = jax.random.fold_in(key, 3)
    values = jnp.clip(jax.random.normal(key, (SAMPLES, TOKENS, D), jnp.float32), -4.0, 4.0)
    return values.astype(jnp.bfloat16)


def draw_key(key, part):
    key = jax.random.fold_in(key, 5)
    values = jnp.clip(jax.random.normal(key, (SAMPLES, TOKENS, D), jnp.float32), -4.0, 4.0)
    return values.astype(jnp.bfloat16)


def draw_table(key, part):
    key = jax.random.fold_in(key, 7)
    block_id = jnp.arange(NBLK, dtype=jnp.int32)
    owner = block_id // BLK_DEV
    place = block_id % BLK_DEV
    span = 3 * BLK_DEV
    noise = jax.random.randint(key, (NBLK, span), 0, 1 << 20, dtype=jnp.int32)
    position = jnp.arange(span, dtype=jnp.int32)
    ranking = noise * 64 + position[None, :]
    ranking = jnp.where(position[None, :] == (BLK_DEV + place)[:, None], -1, ranking)
    chosen_values, picked = lax.top_k(ranking, 3)
    others = jnp.mod((owner[:, None] - 1) * BLK_DEV + picked.astype(jnp.int32), NBLK)
    return jnp.concatenate([block_id[:, None], others], axis=1).astype(jnp.int32)


def block_scale(rng, dims, shards, least, high):
    gain, own = 1.0, jax.random.fold_in(rng, 6)
    for axis_at, blocks in shards:
        steps = jnp.exp(jax.random.uniform(jax.random.fold_in(own, axis_at), (blocks,), jnp.float32, least / len(shards), high / len(shards)))
        gain = gain * jnp.repeat(steps, dims[axis_at] // blocks).reshape([-1 if axis == axis_at else 1 for axis in range(len(dims))])
    return gain


def gaussian(own_key, shape, scale, limit, split=(), kind=jnp.bfloat16):
    loudness = block_scale(own_key, shape, split, -0.22, 0.18) if split else 1.0
    values = jax.random.normal(own_key, shape, jnp.float32) * scale * loudness
    return jnp.minimum(jnp.maximum(values, -limit), limit).astype(kind)


def setup_inputs(seed: int = 0) -> dict:
    key_of = jax.random.split(jax.random.key(seed), 7)
    return {
        "query": draw_query(jax.random.fold_in(key_of[6], 71), 0),
        "key": draw_key(jax.random.fold_in(key_of[6], 71), 0),
        "value": gaussian(key_of[2], (SAMPLES, TOKENS, D), 1.0, 6.0, ((0, 16), (1, 64))),
        "table": draw_table(jax.random.fold_in(key_of[6], 71), 0),
        "out_weight": gaussian(key_of[4], (D, D), D ** -0.5, 0.25),
        "cotangent": gaussian(key_of[5], (SAMPLES, TOKENS, D), 1.0, 6.0, ((0, 16), (1, 64))),
    }


def local_pass(local_query, key_window, value_window, candidate, local_grad):
    block_count = candidate.shape[0]
    width = local_query.shape[1]
    head_size = width // H
    scale = 1.0 / math.sqrt(head_size)
    key_blocks = key_window.reshape(3 * block_count, BS, width)[candidate].reshape(block_count, 4 * BS, H, head_size).astype(jnp.float32)
    value_blocks = value_window.reshape(3 * block_count, BS, width)[candidate].reshape(block_count, 4 * BS, H, head_size).astype(jnp.float32)
    query_blocks = local_query.reshape(block_count, BS, H, head_size).astype(jnp.float32)
    grad_blocks = local_grad.reshape(block_count, BS, H, head_size).astype(jnp.float32)
    scores = jnp.einsum('bqhe,bkhe->bhqk', query_blocks, key_blocks) * scale
    row_max = lax.optimization_barrier(jnp.max(scores, axis=-1, keepdims=True))
    log_total = row_max + jnp.log(lax.optimization_barrier(jnp.sum(jnp.exp(scores - row_max), axis=-1, keepdims=True)))
    weights = jnp.exp(scores - log_total)
    rounded = lax.optimization_barrier(weights.astype(jnp.bfloat16)).astype(jnp.float32)
    attn = jnp.einsum('bhqk,bkhe->bqhe', rounded, value_blocks).astype(jnp.bfloat16).reshape(block_count * BS, width)
    dprob = jnp.einsum('bqhe,bkhe->bhqk', grad_blocks, value_blocks)
    delta = lax.optimization_barrier(jnp.sum(weights * dprob, axis=-1, keepdims=True))
    dscore = lax.optimization_barrier((weights * (dprob - delta) * scale).astype(jnp.bfloat16)).astype(jnp.float32)
    grad_query = jnp.einsum('bhqk,bkhe->bqhe', dscore, key_blocks).astype(jnp.bfloat16).reshape(block_count * BS, width)
    key_terms = jnp.einsum('bhqk,bqhe->bkhe', dscore, query_blocks).reshape(block_count * 4, BS, width)
    value_terms = jnp.einsum('bhqk,bqhe->bkhe', rounded, grad_blocks).reshape(block_count * 4, BS, width)
    selector = (candidate.reshape(-1)[:, None] == jnp.arange(3 * block_count, dtype=jnp.int32)[None, :]).astype(jnp.float32)
    key_window_grad = jnp.einsum('nc,nsf->csf', selector, key_terms, precision=lax.Precision.HIGHEST).reshape(3 * block_count * BS, width)
    value_window_grad = jnp.einsum('nc,nsf->csf', selector, value_terms, precision=lax.Precision.HIGHEST).reshape(3 * block_count * BS, width)
    return (attn, grad_query, key_window_grad, value_window_grad)

def windows(array):
    shaped = array.reshape(N_CTX, TOK_DEV, D)
    return jnp.concatenate([jnp.roll(shaped, 1, 0), shaped, jnp.roll(shaped, -1, 0)], axis=1)

def combine(terms):
    parts = lax.optimization_barrier(terms.reshape(N_CTX, 3, TOK_DEV, D).astype(jnp.bfloat16)).astype(jnp.float32)
    total = jnp.roll(parts[:, 0], -1, 0) + parts[:, 1] + jnp.roll(parts[:, 2], 1, 0)
    return total.astype(jnp.bfloat16).reshape(TOKENS, D)

def reference(query, key, value, table, out_weight, cotangent):
    offsets = (jnp.arange(N_CTX, dtype=jnp.int32) - 1) * BLK_DEV
    candidate = jnp.mod(table.reshape(N_CTX, BLK_DEV, 4).astype(jnp.int32) - offsets[:, None, None], NBLK).astype(jnp.int32)

    def per_sample(items):
        sample_query, sample_key, sample_value, sample_grad = items
        grad_attn = jnp.dot(sample_grad, out_weight.T, preferred_element_type=jnp.float32).astype(jnp.bfloat16)

        def per_device(inputs):
            return local_pass(*inputs)
        attn, grad_q, key_terms, value_terms = lax.map(per_device, (sample_query.reshape(N_CTX, TOK_DEV, D), windows(sample_key), windows(sample_value), candidate, grad_attn.reshape(N_CTX, TOK_DEV, D)))
        attn = attn.reshape(TOKENS, D)
        layer_out = jnp.dot(attn, out_weight, preferred_element_type=jnp.float32).astype(jnp.bfloat16)
        weight_term = jnp.dot(attn.T, sample_grad, preferred_element_type=jnp.float32)
        return (layer_out, grad_q.reshape(TOKENS, D), combine(key_terms), combine(value_terms), weight_term)
    layer_out, grad_query, grad_key, grad_value, weight_terms = lax.map(per_sample, (query, key, value, cotangent))
    grad_weight = lax.optimization_barrier(jnp.sum(weight_terms, axis=0)) / math.sqrt(SAMPLES * TOKENS)
    return (layer_out, grad_query, grad_key, grad_value, grad_weight)
```

```python
import functools
import math

import jax
import jax.numpy as jnp
from jax import lax
from jax.experimental import pallas as pl
from jax.experimental.pallas import tpu as pltpu
from jax.sharding import PartitionSpec as P

MESH = pl.DeviceIdType.MESH
F32 = jnp.float32
BF16 = jnp.bfloat16

NX, NY, NZ, NC = 4, 8, 16, 2
ZLO = 8
TOK = 128
D = 512
BS = 64
PAIRS = 4
WIN = 3 * TOK


def place():
    ctx, dp = lax.axis_index("ctx"), lax.axis_index("dp")
    x = lax.rem(ctx, NX)
    zh = lax.rem(ctx // NX, NZ // ZLO)
    y = ctx // (NX * (NZ // ZLO))
    return ctx, dp, x, y, zh * ZLO + dp // NC, lax.rem(dp, NC)


def at(x, y, z, c):
    return (y * (NX * (NZ // ZLO)) + (z // ZLO) * NX + x, lax.rem(z, ZLO) * NC + c)


def nt(a, b):
    return lax.dot_general(a, b, (((1,), (1,)), ((), ())), preferred_element_type=F32)


def nn(a, b):
    return lax.dot_general(a, b, (((1,), (0,)), ((), ())), preferred_element_type=F32)


def tn(a, b):
    return lax.dot_general(a, b, (((0,), (0,)), ((), ())), preferred_element_type=F32)


def kernel(
    table, q, k, v, w, cot,
    layer_out, grad_q, grad_k, grad_v, grad_w,
    kwin, vwin, g, attn, bias,
    part_out, part_in, own,
    c_out, c_in, c_own, x_out, x_in, x_own, y_out, y_in, y_own, zall, gw,
    kv_s, kv_r, part_s, part_r, c_s, c_r, x_s, x_r, y_s, y_r, z_s, z_r,
    gy_s, gy_r, gx_s, gx_r, gc_s, gc_r,
):
    ctx, dp, x, y, z, c = place()
    n_ctx = lax.axis_size("ctx")
    before = (lax.rem(ctx + n_ctx - 1, n_ctx), dp)
    after = (lax.rem(ctx + 1, n_ctx), dp)
    other = at(x, y, z, 1 - c)
    xs = [lax.rem(x + i, NX) for i in range(NX)]
    ys = [lax.rem(y + i, NY) for i in range(NY)]
    zs = [lax.rem(z + i, NZ) for i in range(NZ)]

    barrier = pltpu.get_barrier_semaphore()
    peers = [before, after, other]
    peers += [at(i, y, z, c) for i in xs[1:]]
    peers += [at(x, i, z, c) for i in ys[1:]]
    peers += [at(x, y, i, c) for i in zs[1:]]
    for peer in peers:
        pl.semaphore_signal(barrier, 1, device_id=peer, device_id_type=MESH)
    pl.semaphore_wait(barrier, len(peers))

    def remote(src, dst, ssem, rsem, to):
        return pltpu.make_async_remote_copy(
            src_ref=src, dst_ref=dst, send_sem=ssem, recv_sem=rsem, device_id=to, device_id_type=MESH
        )

    def lanes(p):
        return pl.ds(p * 128, 128)

    halo = []
    for p in range(PAIRS):
        row = []
        for i, (src, win) in enumerate(((k, kwin), (v, vwin))):
            for j, (to, start) in enumerate(((after, 0), (before, 2 * TOK))):
                row.append(remote(
                    src.at[0, :, lanes(p)], win.at[pl.ds(start, TOK), lanes(p)],
                    kv_s.at[p, i, j], kv_r.at[p, i, j], to,
                ))
        for copy in row:
            copy.start()
        halo.append(row)

    kwin[pl.ds(TOK, TOK), :] = k[0]
    vwin[pl.ds(TOK, TOK), :] = v[0]
    g[...] = nt(cot[0], w[...]).astype(BF16)

    block = lax.broadcasted_iota(jnp.int32, (BS, WIN), 1) // BS
    for b in range(2):
        hit = None
        for j in range(4):
            cand = lax.rem(table[b, j] - (ctx - 1) * 2 + 2 * n_ctx, 2 * n_ctx)
            same = block == cand
            hit = same if hit is None else jnp.logical_or(hit, same)
        rows = jnp.where(hit, 0.0, -1e30).astype(F32)
        bias[pl.ds(b * BS, BS), :] = rows
        bias[pl.ds(TOK + b * BS, BS), :] = rows

    left = lax.broadcasted_iota(jnp.int32, (TOK, 128), 1) < 64

    def split(a):
        zero = jnp.zeros_like(a)
        return jnp.concatenate([jnp.where(left, a, zero), jnp.where(left, zero, a)], axis=0)

    def merged(a):
        return jnp.where(left, a[:TOK], a[TOK:])

    pending = []

    def send(copy):
        copy.start()
        pending.append(copy)

    def attention(p):
        for copy in halo[p]:
            copy.wait_recv()
        l = lanes(p)
        kw, vw = kwin[:, l], vwin[:, l]
        q2 = split(q[0, :, l] * jnp.asarray(0.125, BF16))
        s = nt(q2, kw) + bias[...]
        e = jnp.exp(s - jnp.max(s, axis=1, keepdims=True))
        weights = e * (1.0 / jnp.sum(e, axis=1, keepdims=True))
        rounded = weights.astype(BF16)
        out = merged(nn(rounded, vw)).astype(BF16)
        attn[:, l] = out
        term = tn(out, cot[0])
        c_own[p] = jnp.where(c == 0, term[:, :256], term[:, 256:])
        c_out[p] = jnp.where(c == 0, term[:, 256:], term[:, :256]).astype(BF16)
        send(remote(c_out.at[p], c_in.at[p], c_s.at[p], c_r.at[p], other))

        g2 = split(g[:, l])
        dprob = nt(g2, vw)
        delta = jnp.sum(weights * dprob, axis=1, keepdims=True)
        ds = (weights * (dprob - delta)).astype(BF16)
        dk = tn(ds, q2)
        dv = tn(rounded, g2)
        for i, d in enumerate((dk, dv)):
            part_out[i, 0, :, l] = d[:TOK].astype(BF16)
            part_out[i, 1, :, l] = d[2 * TOK:].astype(BF16)
            own[i, :, l] = d[TOK:2 * TOK]
            for j, to in enumerate((before, after)):
                send(remote(
                    part_out.at[i, j, :, l], part_in.at[i, j, :, l],
                    part_s.at[p, i, j], part_r.at[p, i, j], to,
                ))
        grad_q[0, :, l] = (merged(nn(ds, kw)) * 0.125).astype(BF16)

    def core_step(p):
        remote(c_out.at[p], c_in.at[p], c_s.at[p], c_r.at[p], other).wait_recv()
        total = c_own[p] + c_in[p].astype(F32)
        x_own[p] = total
        x_out[p] = total.astype(BF16)
        for i in range(1, NX):
            send(remote(
                x_out.at[p, pl.ds(xs[i] * 32, 32)], x_in.at[p, i - 1],
                x_s.at[p, i - 1], x_r.at[p, i - 1], at(xs[i], y, z, c),
            ))

    def x_step(p):
        total = x_own[p, pl.ds(x * 32, 32)]
        for i in range(1, NX):
            remote(
                x_out.at[p, pl.ds(xs[i] * 32, 32)], x_in.at[p, i - 1],
                x_s.at[p, i - 1], x_r.at[p, i - 1], at(xs[i], y, z, c),
            ).wait_recv()
            total = total + x_in[p, i - 1].astype(F32)
        y_out[p] = total.astype(BF16)
        for half in range(2):
            owner = 2 * p + half

            @pl.when(y == owner)
            def _():
                y_own[...] = total[half * 16:half * 16 + 16]

            @pl.when(y != owner)
            def _():
                slot = lax.rem(owner - y + NY, NY) - 1
                remote(
                    y_out.at[p, pl.ds(half * 16, 16)], y_in.at[slot],
                    y_s.at[p, half], y_r.at[slot], at(x, owner, z, c),
                ).start()

    def y_step():
        total = y_own[...]
        for i in range(NY - 1):
            remote(y_out.at[0, pl.ds(0, 16)], y_in.at[i], y_s.at[0, 0], y_r.at[i], other).wait_recv()
            total = total + y_in[i].astype(F32)
        zall[z] = total.astype(BF16)
        for i in range(1, NZ):
            send(remote(zall.at[z], zall.at[z], z_s.at[i - 1], z_r.at[z], at(x, y, zs[i], c)))

    def z_step():
        for i in range(1, NZ):
            remote(zall.at[z], zall.at[zs[i]], z_s.at[0], z_r.at[zs[i]], other).wait_recv()
        total = zall[0].astype(F32)
        for i in range(1, NZ):
            total = total + zall[i].astype(F32)
        gw[c, x, y] = total.astype(BF16)
        for i in range(1, NY):
            send(remote(gw.at[c, x, y], gw.at[c, x, y], gy_s.at[i - 1], gy_r.at[y], at(x, ys[i], z, c)))

    def gather_x():
        for i in range(1, NY):
            remote(gw.at[c, x, y], gw.at[c, x, ys[i]], gy_s.at[0], gy_r.at[ys[i]], other).wait_recv()
        for i in range(1, NX):
            send(remote(gw.at[c, x], gw.at[c, x], gx_s.at[i - 1], gx_r.at[x], at(xs[i], y, z, c)))

    def gather_core():
        for i in range(1, NX):
            remote(gw.at[c, x], gw.at[c, xs[i]], gx_s.at[0], gx_r.at[xs[i]], other).wait_recv()
        send(remote(gw.at[c], gw.at[c], gc_s, gc_r, other))

    attention(0)
    attention(1)
    core_step(0)
    attention(2)
    core_step(1)
    x_step(0)
    attention(3)
    core_step(2)
    x_step(1)
    core_step(3)
    x_step(2)
    x_step(3)
    y_step()
    layer_out[0] = nn(attn[...], w[...]).astype(BF16)
    z_step()
    gather_x()
    gather_core()

    for p in range(PAIRS):
        for i in range(2):
            for j, to in enumerate((before, after)):
                remote(
                    part_out.at[i, j, :, lanes(p)], part_in.at[i, j, :, lanes(p)],
                    part_s.at[p, i, j], part_r.at[p, i, j], to,
                ).wait_recv()
    for i, out in enumerate((grad_k, grad_v)):
        out[0] = (own[i] + part_in[i, 0].astype(F32) + part_in[i, 1].astype(F32)).astype(BF16)

    remote(gw.at[c], gw.at[1 - c], gc_s, gc_r, other).wait_recv()
    scale = 1.0 / math.sqrt(TOK * NX * NY * NZ * NC)
    for ci in range(NC):
        for yi in range(NY):
            for xi in range(NX):
                row = (yi // 2) * 128 + xi * 32 + (yi % 2) * 16
                grad_w[row:row + 16, ci * 256:ci * 256 + 256] = gw[ci, xi, yi].astype(F32) * scale

    for row in halo:
        for copy in row:
            copy.wait_send()
    for copy in pending:
        copy.wait_send()
    for p in range(PAIRS):
        for half in range(2):
            @pl.when(y != 2 * p + half)
            def _():
                remote(
                    y_out.at[p, pl.ds(half * 16, 16)], y_in.at[0],
                    y_s.at[p, half], y_r.at[0], other,
                ).wait_send()


def body(query, key, value, table, out_weight, cotangent):
    vmem = pl.BlockSpec(memory_space=pltpu.VMEM)
    dma = pltpu.SemaphoreType.DMA
    like = jax.ShapeDtypeStruct((1, TOK, D), BF16)
    return pl.pallas_call(
        kernel,
        out_shape=(like, like, like, like, jax.ShapeDtypeStruct((D, D), F32)),
        in_specs=[pl.BlockSpec(memory_space=pltpu.SMEM)] + [vmem] * 5,
        out_specs=(vmem,) * 5,
        scratch_shapes=[
            pltpu.VMEM((WIN, D), BF16), pltpu.VMEM((WIN, D), BF16),
            pltpu.VMEM((TOK, D), BF16), pltpu.VMEM((TOK, D), BF16), pltpu.VMEM((2 * TOK, WIN), F32),
            pltpu.VMEM((2, 2, TOK, D), BF16), pltpu.VMEM((2, 2, TOK, D), BF16), pltpu.VMEM((2, TOK, D), F32),
            pltpu.VMEM((PAIRS, 128, 256), BF16), pltpu.VMEM((PAIRS, 128, 256), BF16), pltpu.VMEM((PAIRS, 128, 256), F32),
            pltpu.VMEM((PAIRS, 128, 256), BF16), pltpu.VMEM((PAIRS, NX - 1, 32, 256), BF16), pltpu.VMEM((PAIRS, 128, 256), F32),
            pltpu.VMEM((PAIRS, 32, 256), BF16), pltpu.VMEM((NY - 1, 16, 256), BF16), pltpu.VMEM((16, 256), F32),
            pltpu.VMEM((NZ, 16, 256), BF16), pltpu.VMEM((NC, NX, NY, 16, 256), BF16),
            dma((PAIRS, 2, 2)), dma((PAIRS, 2, 2)), dma((PAIRS, 2, 2)), dma((PAIRS, 2, 2)),
            dma((PAIRS,)), dma((PAIRS,)), dma((PAIRS, NX - 1)), dma((PAIRS, NX - 1)),
            dma((PAIRS, 2)), dma((NY - 1,)), dma((NZ - 1,)), dma((NZ,)),
            dma((NY - 1,)), dma((NY,)), dma((NX - 1,)), dma((NX,)), dma, dma,
        ],
        compiler_params=pltpu.CompilerParams(
            collective_id=0, has_side_effects=True, vmem_limit_bytes=32 * 2**20
        ),
    )(table, query, key, value, out_weight, cotangent)


def solution(mesh):
    rows = P("dp", "ctx", None)
    return jax.shard_map(
        body,
        mesh=mesh,
        in_specs=(rows, rows, rows, P("ctx", None), P(), rows),
        out_specs=(rows, rows, rows, rows, P()),
        check_vma=False,
    )
```

```python
import functools
import math

import jax
import jax.numpy as jnp
from jax import lax
from jax.experimental import pallas as pl
from jax.experimental.pallas import tpu as pltpu
from jax.sharding import PartitionSpec as P

MESH = pl.DeviceIdType.MESH
F32 = jnp.float32
BF16 = jnp.bfloat16

NX, NY, NZ, NC = 4, 8, 16, 2
ZLO = 8
TOK = 128
D = 512
BS = 64
PAIRS = 4
WIN = 3 * TOK


def place():
    ctx, dp = lax.axis_index("ctx"), lax.axis_index("dp")
    x = lax.rem(ctx, NX)
    zh = lax.rem(ctx // NX, NZ // ZLO)
    y = ctx // (NX * (NZ // ZLO))
    return ctx, dp, x, y, zh * ZLO + dp // NC, lax.rem(dp, NC)


def at(x, y, z, c):
    return (y * (NX * (NZ // ZLO)) + (z // ZLO) * NX + x, lax.rem(z, ZLO) * NC + c)


def nt(a, b):
    return lax.dot_general(a, b, (((1,), (1,)), ((), ())), preferred_element_type=F32)


def nn(a, b):
    return lax.dot_general(a, b, (((1,), (0,)), ((), ())), preferred_element_type=F32)


def tn(a, b):
    return lax.dot_general(a, b, (((0,), (0,)), ((), ())), preferred_element_type=F32)


def kernel(
    table_in, q_in, k_in, v_in, w_in, cot_in,
    layer_out, grad_q, grad_k, grad_v, gw,
    table, q, w, cot, kwin, vwin, g, attn, bias,
    part_out, part_in, own,
    c_out, c_in, c_own, x_out, x_in, x_own, y_out, y_in, y_own, zall,
    relay, in_s, kv_s, kv_r, fwd_s, to_relay_s, relay_r, relay_s, part_s, part_r, c_s, c_r, x_s, x_r, y_s, y_r, z_s, z_r,
    gy_s, gy_r, gx_s, gx_r, gc_s, gc_r,
):
    ctx, dp, x, y, z, c = place()
    n_ctx = lax.axis_size("ctx")
    before = (lax.rem(ctx + n_ctx - 1, n_ctx), dp)
    after = (lax.rem(ctx + 1, n_ctx), dp)
    other = at(x, y, z, 1 - c)
    xs = [lax.rem(x + i, NX) for i in range(NX)]
    ys = [lax.rem(y + i, NY) for i in range(NY)]
    zs = [lax.rem(z + i, NZ) for i in range(NZ)]

    first, second, third, last = x == 0, x == 1, x == 2, x == NX - 1
    far = jnp.where(x < 2, lax.rem(ctx + n_ctx - 2, n_ctx), lax.rem(ctx + 2, n_ctx)), dp

    barrier = pltpu.get_barrier_semaphore()
    peers = [before, after, far]
    peers += [at(x, y, i, c) for i in zs[1:]]
    peers += [at(x, i, z, c) for i in ys[1:]]
    peers += [at(i, y, z, c) for i in xs[1:]]
    peers += [other]
    for peer in peers:
        pl.semaphore_signal(barrier, 1, device_id=peer, device_id_type=MESH)
    loads = []
    for i, (src, dst) in enumerate((
        (k_in.at[0], kwin.at[pl.ds(TOK, TOK)]), (v_in.at[0], vwin.at[pl.ds(TOK, TOK)]),
        (cot_in.at[0], cot.at[0]), (w_in, w), (q_in.at[0], q.at[0]), (table_in, table),
    )):
        copy = pltpu.make_async_copy(src, dst, in_s.at[i])
        copy.start()
        loads.append(copy)
    pl.semaphore_wait(barrier, len(peers))

    def remote(src, dst, ssem, rsem, to):
        return pltpu.make_async_remote_copy(
            src_ref=src, dst_ref=dst, send_sem=ssem, recv_sem=rsem, device_id=to, device_id_type=MESH
        )

    def lanes(p):
        return pl.ds(p * 128, 128)

    wins = (kwin, vwin)
    starts = (0, 2 * TOK)

    def halo(p, i, j):
        return remote(
            (k_in, v_in)[i].at[0, :, lanes(p)], wins[i].at[pl.ds(starts[j], TOK), lanes(p)],
            kv_s.at[p, i, j], kv_r.at[p, i, j], (after, before)[j],
        )

    def handed_on(p, j):
        rows = wins[1].at[pl.ds(starts[1 - j], TOK), lanes(p)]
        return remote(rows, wins[1].at[pl.ds(starts[j], TOK), lanes(p)], fwd_s.at[p], kv_r.at[p, 1, j], far)

    for p in range(PAIRS):
        halo(p, 0, 0).start()
        halo(p, 0, 1).start()

        @pl.when(jnp.logical_not(last))
        def _():
            halo(p, 1, 0).start()

        @pl.when(jnp.logical_not(first))
        def _():
            halo(p, 1, 1).start()

    for copy in loads:
        copy.wait()
    g[...] = nt(cot[0], w[...]).astype(BF16)

    block = lax.broadcasted_iota(jnp.int32, (BS, WIN), 1) // BS
    for b in range(2):
        hit = None
        for j in range(4):
            cand = lax.rem(table[b, j] - (ctx - 1) * 2 + 2 * n_ctx, 2 * n_ctx)
            same = block == cand
            hit = same if hit is None else jnp.logical_or(hit, same)
        rows = jnp.where(hit, 0.0, -1e30).astype(F32)
        bias[pl.ds(b * BS, BS), :] = rows
        bias[pl.ds(TOK + b * BS, BS), :] = rows

    left = lax.broadcasted_iota(jnp.int32, (TOK, 128), 1) < 64

    def split(a):
        zero = jnp.zeros_like(a)
        return jnp.concatenate([jnp.where(left, a, zero), jnp.where(left, zero, a)], axis=0)

    def merged(a):
        return jnp.where(left, a[:TOK], a[TOK:])

    pending = []

    def send(copy):
        copy.start()
        pending.append(copy)

    @pl.when(third)
    def _():
        for p in range(PAIRS):
            halo(p, 1, 1).wait_recv()
            handed_on(p, 0).start()

    @pl.when(second)
    def _():
        for p in range(PAIRS):
            halo(p, 1, 0).wait_recv()
            handed_on(p, 1).start()

    def part(p, i, j):
        return remote(
            part_out.at[i, j, :, lanes(p)], part_in.at[i, j, :, lanes(p)],
            part_s.at[p, i, j], part_r.at[p, i, j], (before, after)[j],
        )

    def to_relay(p, j):
        return remote(
            part_out.at[1, j, :, lanes(p)], relay.at[:, lanes(p)],
            to_relay_s.at[p], relay_r.at[p], (after, before)[j],
        )

    def from_relay(p, j):
        return remote(
            relay.at[:, lanes(p)], part_in.at[1, j, :, lanes(p)], relay_s.at[p], part_r.at[p, 1, j], far
        )

    def hand_on_part(p):
        @pl.when(third)
        def _():
            to_relay(p, 1).wait_recv()
            from_relay(p, 1).start()

        @pl.when(second)
        def _():
            to_relay(p, 0).wait_recv()
            from_relay(p, 0).start()

    def attention(p):
        halo(p, 0, 0).wait_recv()
        halo(p, 0, 1).wait_recv()

        @pl.when(jnp.logical_not(second))
        def _():
            halo(p, 1, 0).wait_recv()

        @pl.when(jnp.logical_not(third))
        def _():
            halo(p, 1, 1).wait_recv()

        l = lanes(p)
        kw, vw = kwin[:, l], vwin[:, l]
        q2 = split(q[0, :, l] * jnp.asarray(0.125, BF16))
        s = nt(q2, kw) + bias[...]
        e = jnp.exp(s - jnp.max(s, axis=1, keepdims=True))
        weights = e * (1.0 / jnp.sum(e, axis=1, keepdims=True))
        rounded = weights.astype(BF16)
        out = merged(nn(rounded, vw)).astype(BF16)
        attn[:, l] = out
        term = tn(out, cot[0])
        c_own[p] = jnp.where(c == 0, term[:, :256], term[:, 256:])
        c_out[p] = jnp.where(c == 0, term[:, 256:], term[:, :256]).astype(BF16)
        send(remote(c_out.at[p], c_in.at[p], c_s.at[p], c_r.at[p], other))

        g2 = split(g[:, l])
        dprob = nt(g2, vw)
        delta = jnp.sum(weights * dprob, axis=1, keepdims=True)
        ds = (weights * (dprob - delta)).astype(BF16)
        dk = tn(ds, q2)
        dv = tn(rounded, g2)
        for i, d in enumerate((dk, dv)):
            part_out[i, 0, :, l] = d[:TOK].astype(BF16)
            part_out[i, 1, :, l] = d[2 * TOK:].astype(BF16)
            own[i, :, l] = d[TOK:2 * TOK]
        part(p, 0, 0).start()
        part(p, 0, 1).start()

        @pl.when(first)
        def _():
            to_relay(p, 0).start()

        @pl.when(jnp.logical_not(first))
        def _():
            part(p, 1, 0).start()

        @pl.when(last)
        def _():
            to_relay(p, 1).start()

        @pl.when(jnp.logical_not(last))
        def _():
            part(p, 1, 1).start()

        grad_q[0, :, l] = (merged(nn(ds, kw)) * 0.125).astype(BF16)

    def core_step(p):
        remote(c_out.at[p], c_in.at[p], c_s.at[p], c_r.at[p], other).wait_recv()
        total = c_own[p] + c_in[p].astype(F32)
        x_own[p] = total
        x_out[p] = total.astype(BF16)
        for i in range(1, NX):
            send(remote(
                x_out.at[p, pl.ds(xs[i] * 32, 32)], x_in.at[p, i - 1],
                x_s.at[p, i - 1], x_r.at[p, i - 1], at(xs[i], y, z, c),
            ))

    def x_step(p):
        total = x_own[p, pl.ds(x * 32, 32)]
        for i in range(1, NX):
            remote(
                x_out.at[p, pl.ds(xs[i] * 32, 32)], x_in.at[p, i - 1],
                x_s.at[p, i - 1], x_r.at[p, i - 1], at(xs[i], y, z, c),
            ).wait_recv()
            total = total + x_in[p, i - 1].astype(F32)
        y_out[p] = total.astype(BF16)
        for half in range(2):
            owner = 2 * p + half

            @pl.when(y == owner)
            def _():
                y_own[...] = total[half * 16:half * 16 + 16]

            @pl.when(y != owner)
            def _():
                slot = lax.rem(owner - y + NY, NY) - 1
                remote(
                    y_out.at[p, pl.ds(half * 16, 16)], y_in.at[slot],
                    y_s.at[p, half], y_r.at[slot], at(x, owner, z, c),
                ).start()

    def y_step():
        total = y_own[...]
        for i in range(NY - 1):
            remote(y_out.at[0, pl.ds(0, 16)], y_in.at[i], y_s.at[0, 0], y_r.at[i], other).wait_recv()
            total = total + y_in[i].astype(F32)
        zall[z] = total.astype(BF16)
        for i in range(1, NZ):
            send(remote(zall.at[z], zall.at[z], z_s.at[i - 1], z_r.at[z], at(x, y, zs[i], c)))

    def z_step():
        for i in range(1, NZ):
            remote(zall.at[z], zall.at[zs[i]], z_s.at[0], z_r.at[zs[i]], other).wait_recv()
        total = zall[0].astype(F32)
        for i in range(1, NZ):
            total = total + zall[i].astype(F32)
        gw[c, x, y] = total.astype(BF16)
        for i in range(1, NY):
            send(remote(gw.at[c, x, y], gw.at[c, x, y], gy_s.at[i - 1], gy_r.at[y], at(x, ys[i], z, c)))

    def gather_x():
        for i in range(1, NY):
            remote(gw.at[c, x, y], gw.at[c, x, ys[i]], gy_s.at[0], gy_r.at[ys[i]], other).wait_recv()
        for i in range(1, NX):
            send(remote(gw.at[c, x], gw.at[c, x], gx_s.at[i - 1], gx_r.at[x], at(xs[i], y, z, c)))

    def gather_core():
        for i in range(1, NX):
            remote(gw.at[c, x], gw.at[c, xs[i]], gx_s.at[0], gx_r.at[xs[i]], other).wait_recv()
        send(remote(gw.at[c], gw.at[c], gc_s, gc_r, other))

    attention(0)
    attention(1)
    hand_on_part(0)
    core_step(0)
    attention(2)
    hand_on_part(1)
    core_step(1)
    x_step(0)
    attention(3)
    hand_on_part(2)
    core_step(2)
    x_step(1)
    hand_on_part(3)
    core_step(3)
    x_step(2)
    x_step(3)
    y_step()
    layer_out[0] = nn(attn[...], w[...]).astype(BF16)
    z_step()
    gather_x()
    gather_core()

    for p in range(PAIRS):
        for i in range(2):
            for j in range(2):
                part(p, i, j).wait_recv()
    for i, out in enumerate((grad_k, grad_v)):
        out[0] = (own[i] + part_in[i, 0].astype(F32) + part_in[i, 1].astype(F32)).astype(BF16)

    remote(gw.at[c], gw.at[1 - c], gc_s, gc_r, other).wait_recv()
    for p in range(PAIRS):
        for j in range(2):
            halo(p, 0, j).wait_send()
            part(p, 0, j).wait_send()

        @pl.when(first)
        def _():
            halo(p, 1, 0).wait_send()
            part(p, 1, 1).wait_send()
            to_relay(p, 0).wait_send()

        @pl.when(last)
        def _():
            halo(p, 1, 1).wait_send()
            part(p, 1, 0).wait_send()
            to_relay(p, 1).wait_send()

        @pl.when(jnp.logical_or(second, third))
        def _():
            for j in range(2):
                halo(p, 1, j).wait_send()
                part(p, 1, j).wait_send()
            handed_on(p, 0).wait_send()
            from_relay(p, 0).wait_send()

    for copy in pending:
        copy.wait_send()
    for p in range(PAIRS):
        for half in range(2):
            @pl.when(y != 2 * p + half)
            def _():
                remote(
                    y_out.at[p, pl.ds(half * 16, 16)], y_in.at[0],
                    y_s.at[p, half], y_r.at[0], other,
                ).wait_send()


def finish(layer_out_in, grad_q_in, grad_k_in, grad_v_in, gw, layer_out, grad_q, grad_k, grad_v, grad_w):
    layer_out[...] = layer_out_in[...]
    grad_q[...] = grad_q_in[...]
    grad_k[...] = grad_k_in[...]
    grad_v[...] = grad_v_in[...]
    scale = 1.0 / math.sqrt(TOK * NX * NY * NZ * NC)
    for ci in range(NC):
        for yi in range(NY):
            for xi in range(NX):
                row = (yi // 2) * 128 + xi * 32 + (yi % 2) * 16
                grad_w[row:row + 16, ci * 256:ci * 256 + 256] = gw[ci, xi, yi].astype(F32) * scale


def body(query, key, value, table, out_weight, cotangent):
    vmem = pl.BlockSpec(memory_space=pltpu.VMEM)
    dma = pltpu.SemaphoreType.DMA
    like = jax.ShapeDtypeStruct((1, TOK, D), BF16)
    shapes = (like, like, like, like)
    anywhere = pl.BlockSpec(memory_space=pl.ANY)
    raw = pl.pallas_call(
        kernel,
        out_shape=shapes + (jax.ShapeDtypeStruct((NC, NX, NY, 16, 256), BF16),),
        in_specs=[anywhere] * 6,
        out_specs=(vmem,) * 5,
        scratch_shapes=[
            pltpu.SMEM((2, 4), jnp.int32),
            pltpu.VMEM((1, TOK, D), BF16), pltpu.VMEM((D, D), BF16), pltpu.VMEM((1, TOK, D), BF16),
            pltpu.VMEM((WIN, D), BF16), pltpu.VMEM((WIN, D), BF16),
            pltpu.VMEM((TOK, D), BF16), pltpu.VMEM((TOK, D), BF16), pltpu.VMEM((2 * TOK, WIN), F32),
            pltpu.VMEM((2, 2, TOK, D), BF16), pltpu.VMEM((2, 2, TOK, D), BF16), pltpu.VMEM((2, TOK, D), F32),
            pltpu.VMEM((PAIRS, 128, 256), BF16), pltpu.VMEM((PAIRS, 128, 256), BF16), pltpu.VMEM((PAIRS, 128, 256), F32),
            pltpu.VMEM((PAIRS, 128, 256), BF16), pltpu.VMEM((PAIRS, NX - 1, 32, 256), BF16), pltpu.VMEM((PAIRS, 128, 256), F32),
            pltpu.VMEM((PAIRS, 32, 256), BF16), pltpu.VMEM((NY - 1, 16, 256), BF16), pltpu.VMEM((16, 256), F32),
            pltpu.VMEM((NZ, 16, 256), BF16),
            pltpu.VMEM((TOK, D), BF16), dma((6,)), dma((PAIRS, 2, 2)), dma((PAIRS, 2, 2)),
            dma((PAIRS,)), dma((PAIRS,)), dma((PAIRS,)), dma((PAIRS,)),
            dma((PAIRS, 2, 2)), dma((PAIRS, 2, 2)),
            dma((PAIRS,)), dma((PAIRS,)), dma((PAIRS, NX - 1)), dma((PAIRS, NX - 1)),
            dma((PAIRS, 2)), dma((NY - 1,)), dma((NZ - 1,)), dma((NZ,)),
            dma((NY - 1,)), dma((NY,)), dma((NX - 1,)), dma((NX,)), dma, dma,
        ],
        compiler_params=pltpu.CompilerParams(collective_id=0, has_side_effects=True),
    )(table, query, key, value, out_weight, cotangent)
    return tuple(pl.pallas_call(
        finish,
        out_shape=shapes + (jax.ShapeDtypeStruct((D, D), F32),),
        in_specs=[vmem] * 5,
        out_specs=(vmem,) * 5,
    )(*raw))


def solution(mesh):
    rows = P("dp", "ctx", None)
    return jax.shard_map(
        body,
        mesh=mesh,
        in_specs=(rows, rows, rows, P("ctx", None), P(), rows),
        out_specs=(rows, rows, rows, rows, P()),
        check_vma=False,
    )
```

```python
import functools
import math

import jax
import jax.numpy as jnp
from jax import lax
from jax.experimental import pallas as pl
from jax.experimental.pallas import tpu as pltpu
from jax.sharding import PartitionSpec as P

MESH = pl.DeviceIdType.MESH
F32 = jnp.float32
BF16 = jnp.bfloat16

NX, NY, NZ, NC = 4, 8, 16, 2
ZLO = 8
TOK = 128
D = 512
BS = 64
PAIRS = 4
WIN = 3 * TOK


def place():
    ctx, dp = lax.axis_index("ctx"), lax.axis_index("dp")
    x = lax.rem(ctx, NX)
    zh = lax.rem(ctx // NX, NZ // ZLO)
    y = ctx // (NX * (NZ // ZLO))
    return ctx, dp, x, y, zh * ZLO + dp // NC, lax.rem(dp, NC)


def at(x, y, z, c):
    return (y * (NX * (NZ // ZLO)) + (z // ZLO) * NX + x, lax.rem(z, ZLO) * NC + c)


def nt(a, b):
    return lax.dot_general(a, b, (((1,), (1,)), ((), ())), preferred_element_type=F32)


def nn(a, b):
    return lax.dot_general(a, b, (((1,), (0,)), ((), ())), preferred_element_type=F32)


def tn(a, b):
    return lax.dot_general(a, b, (((0,), (0,)), ((), ())), preferred_element_type=F32)


def kernel(
    table_in, q_in, k_in, v_in, w_in, cot_in,
    layer_out, grad_q, grad_k, grad_v, gw,
    table, q, w, cot, kwin, vwin, g, attn, bias,
    part_out, part_in, own,
    c_out, c_in, c_own, x_out, x_in, x_own, y_out, y_in, y_own, zall,
    relay, in_s, kv_s, kv_r, fwd_s, to_relay_s, relay_r, relay_s, part_s, part_r, c_s, c_r, x_s, x_r, y_s, y_r, z_s, z_r,
    gy_s, gy_r, gx_s, gx_r, gc_s, gc_r,
):
    ctx, dp, x, y, z, c = place()
    n_ctx = lax.axis_size("ctx")
    before = (lax.rem(ctx + n_ctx - 1, n_ctx), dp)
    after = (lax.rem(ctx + 1, n_ctx), dp)
    other = at(x, y, z, 1 - c)
    xs = [lax.rem(x + i, NX) for i in range(NX)]
    ys = [lax.rem(y + i, NY) for i in range(NY)]
    zs = [lax.rem(z + i, NZ) for i in range(NZ)]
    x_away = sorted(range(1, NX), key=lambda i: -min(i, NX - i))
    y_away = sorted(range(1, NY), key=lambda i: -min(i, NY - i))
    z_away = sorted(range(1, NZ), key=lambda i: -min(i, NZ - i))

    first, second, third, last = x == 0, x == 1, x == 2, x == NX - 1
    far = jnp.where(x < 2, lax.rem(ctx + n_ctx - 2, n_ctx), lax.rem(ctx + 2, n_ctx)), dp

    barrier = pltpu.get_barrier_semaphore()
    peers = [before, after, far]
    peers += [at(x, y, zs[i], c) for i in z_away]
    peers += [at(x, ys[i], z, c) for i in y_away]
    peers += [at(xs[i], y, z, c) for i in x_away]
    peers += [other]
    for peer in peers:
        pl.semaphore_signal(barrier, 1, device_id=peer, device_id_type=MESH)
    loads = []
    for i, (src, dst) in enumerate((
        (k_in.at[0], kwin.at[pl.ds(TOK, TOK)]), (v_in.at[0], vwin.at[pl.ds(TOK, TOK)]),
        (cot_in.at[0], cot.at[0]), (w_in, w), (q_in.at[0], q.at[0]), (table_in, table),
    )):
        copy = pltpu.make_async_copy(src, dst, in_s.at[i])
        copy.start()
        loads.append(copy)
    pl.semaphore_wait(barrier, len(peers))

    def remote(src, dst, ssem, rsem, to):
        return pltpu.make_async_remote_copy(
            src_ref=src, dst_ref=dst, send_sem=ssem, recv_sem=rsem, device_id=to, device_id_type=MESH
        )

    def lanes(p):
        return pl.ds(p * 128, 128)

    wins = (kwin, vwin)
    starts = (0, 2 * TOK)

    def halo(p, i, j):
        return remote(
            (k_in, v_in)[i].at[0, :, lanes(p)], wins[i].at[pl.ds(starts[j], TOK), lanes(p)],
            kv_s.at[p, i, j], kv_r.at[p, i, j], (after, before)[j],
        )

    def handed_on(p, j):
        rows = wins[1].at[pl.ds(starts[1 - j], TOK), lanes(p)]
        return remote(rows, wins[1].at[pl.ds(starts[j], TOK), lanes(p)], fwd_s.at[p], kv_r.at[p, 1, j], far)

    for p in range(PAIRS):
        halo(p, 0, 0).start()
        halo(p, 0, 1).start()

        @pl.when(jnp.logical_not(last))
        def _():
            halo(p, 1, 0).start()

        @pl.when(jnp.logical_not(first))
        def _():
            halo(p, 1, 1).start()

    for copy in loads:
        copy.wait()
    g[...] = nt(cot[0], w[...]).astype(BF16)

    block = lax.broadcasted_iota(jnp.int32, (BS, WIN), 1) // BS
    for b in range(2):
        hit = None
        for j in range(4):
            cand = lax.rem(table[b, j] - (ctx - 1) * 2 + 2 * n_ctx, 2 * n_ctx)
            same = block == cand
            hit = same if hit is None else jnp.logical_or(hit, same)
        rows = jnp.where(hit, 0.0, -1e30).astype(F32)
        bias[pl.ds(b * BS, BS), :] = rows
        bias[pl.ds(TOK + b * BS, BS), :] = rows

    left = lax.broadcasted_iota(jnp.int32, (TOK, 128), 1) < 64

    def split(a):
        zero = jnp.zeros_like(a)
        return jnp.concatenate([jnp.where(left, a, zero), jnp.where(left, zero, a)], axis=0)

    def merged(a):
        return jnp.where(left, a[:TOK], a[TOK:])

    pending = []

    def send(copy):
        copy.start()
        pending.append(copy)

    @pl.when(third)
    def _():
        for p in range(PAIRS):
            halo(p, 1, 1).wait_recv()
            handed_on(p, 0).start()

    @pl.when(second)
    def _():
        for p in range(PAIRS):
            halo(p, 1, 0).wait_recv()
            handed_on(p, 1).start()

    def part(p, i, j):
        return remote(
            part_out.at[i, j, :, lanes(p)], part_in.at[i, j, :, lanes(p)],
            part_s.at[p, i, j], part_r.at[p, i, j], (before, after)[j],
        )

    def to_relay(p, j):
        return remote(
            part_out.at[1, j, :, lanes(p)], relay.at[:, lanes(p)],
            to_relay_s.at[p], relay_r.at[p], (after, before)[j],
        )

    def from_relay(p, j):
        return remote(
            relay.at[:, lanes(p)], part_in.at[1, j, :, lanes(p)], relay_s.at[p], part_r.at[p, 1, j], far
        )

    def hand_on_part(p):
        @pl.when(third)
        def _():
            to_relay(p, 1).wait_recv()
            from_relay(p, 1).start()

        @pl.when(second)
        def _():
            to_relay(p, 0).wait_recv()
            from_relay(p, 0).start()

    def attention(p):
        halo(p, 0, 0).wait_recv()
        halo(p, 0, 1).wait_recv()

        @pl.when(jnp.logical_not(second))
        def _():
            halo(p, 1, 0).wait_recv()

        @pl.when(jnp.logical_not(third))
        def _():
            halo(p, 1, 1).wait_recv()

        l = lanes(p)
        kw, vw = kwin[:, l], vwin[:, l]
        q2 = split(q[0, :, l] * jnp.asarray(0.125, BF16))
        s = nt(q2, kw) + bias[...]
        e = jnp.exp(s - jnp.max(s, axis=1, keepdims=True))
        weights = e * (1.0 / jnp.sum(e, axis=1, keepdims=True))
        rounded = weights.astype(BF16)
        out = merged(nn(rounded, vw)).astype(BF16)
        attn[:, l] = out
        term = tn(out, cot[0])
        c_own[p] = jnp.where(c == 0, term[:, :256], term[:, 256:])
        c_out[p] = jnp.where(c == 0, term[:, 256:], term[:, :256]).astype(BF16)
        send(remote(c_out.at[p], c_in.at[p], c_s.at[p], c_r.at[p], other))

        g2 = split(g[:, l])
        dprob = nt(g2, vw)
        delta = jnp.sum(weights * dprob, axis=1, keepdims=True)
        ds = (weights * (dprob - delta)).astype(BF16)
        dk = tn(ds, q2)
        dv = tn(rounded, g2)
        for i, d in enumerate((dk, dv)):
            part_out[i, 0, :, l] = d[:TOK].astype(BF16)
            part_out[i, 1, :, l] = d[2 * TOK:].astype(BF16)
            own[i, :, l] = d[TOK:2 * TOK]
        grad_q[0, :, l] = (merged(nn(ds, kw)) * 0.125).astype(BF16)

    def send_parts(p):
        part(p, 0, 0).start()
        part(p, 0, 1).start()

        @pl.when(first)
        def _():
            to_relay(p, 0).start()

        @pl.when(jnp.logical_not(first))
        def _():
            part(p, 1, 0).start()

        @pl.when(last)
        def _():
            to_relay(p, 1).start()

        @pl.when(jnp.logical_not(last))
        def _():
            part(p, 1, 1).start()

    def core_step(p):
        remote(c_out.at[p], c_in.at[p], c_s.at[p], c_r.at[p], other).wait_recv()
        total = c_own[p] + c_in[p].astype(F32)
        x_own[p] = total
        x_out[p] = total.astype(BF16)
        for i in x_away:
            send(remote(
                x_out.at[p, pl.ds(xs[i] * 32, 32)], x_in.at[p, i - 1],
                x_s.at[p, i - 1], x_r.at[p, i - 1], at(xs[i], y, z, c),
            ))

    def x_step(p):
        total = x_own[p, pl.ds(x * 32, 32)]
        for i in range(1, NX):
            remote(
                x_out.at[p, pl.ds(xs[i] * 32, 32)], x_in.at[p, i - 1],
                x_s.at[p, i - 1], x_r.at[p, i - 1], at(xs[i], y, z, c),
            ).wait_recv()
            total = total + x_in[p, i - 1].astype(F32)
        y_out[p] = total.astype(BF16)
        for half in range(2):
            owner = 2 * p + half

            @pl.when(y == owner)
            def _():
                y_own[...] = total[half * 16:half * 16 + 16]

            @pl.when(y != owner)
            def _():
                slot = lax.rem(owner - y + NY, NY) - 1
                remote(
                    y_out.at[p, pl.ds(half * 16, 16)], y_in.at[slot],
                    y_s.at[p, half], y_r.at[slot], at(x, owner, z, c),
                ).start()

    def owns(p):
        return jnp.logical_or(y == 2 * p, y == 2 * p + 1)

    def to_z(i):
        return remote(zall.at[z], zall.at[z], z_s.at[i - 1], z_r.at[z], at(x, y, zs[i], c))

    def to_y(i):
        return remote(gw.at[c, x, y], gw.at[c, x, y], gy_s.at[i - 1], gy_r.at[y], at(x, ys[i], z, c))

    def y_step(p):
        @pl.when(owns(p))
        def _():
            total = y_own[...]
            for i in range(NY - 1):
                remote(y_out.at[0, pl.ds(0, 16)], y_in.at[i], y_s.at[0, 0], y_r.at[i], other).wait_recv()
                total = total + y_in[i].astype(F32)
            zall[z] = total.astype(BF16)
            for i in z_away:
                to_z(i).start()

    def z_step(p):
        @pl.when(owns(p))
        def _():
            for i in range(1, NZ):
                remote(zall.at[z], zall.at[zs[i]], z_s.at[0], z_r.at[zs[i]], other).wait_recv()
            total = zall[0].astype(F32)
            for i in range(1, NZ):
                total = total + zall[i].astype(F32)
            gw[c, x, y] = total.astype(BF16)
            for i in y_away:
                to_y(i).start()

    def gather_x(p):
        for yi in (2 * p, 2 * p + 1):
            @pl.when(y != yi)
            def _():
                remote(gw.at[c, x, y], gw.at[c, x, yi], gy_s.at[0], gy_r.at[yi], other).wait_recv()

            for i in x_away:
                send(remote(
                    gw.at[c, x, yi], gw.at[c, x, yi], gx_s.at[yi, i - 1], gx_r.at[yi, x], at(xs[i], y, z, c)
                ))

    def gather_core(p):
        for yi in (2 * p, 2 * p + 1):
            for i in range(1, NX):
                remote(
                    gw.at[c, x, yi], gw.at[c, xs[i], yi], gx_s.at[yi, 0], gx_r.at[yi, xs[i]], other
                ).wait_recv()
            send(remote(gw.at[c, :, yi], gw.at[c, :, yi], gc_s.at[yi], gc_r.at[yi], other))

    attention(0)
    send_parts(0)
    attention(1)
    send_parts(1)
    attention(2)
    send_parts(2)
    attention(3)
    send_parts(3)
    core_step(0)
    core_step(1)
    core_step(2)
    core_step(3)
    hand_on_part(0)
    hand_on_part(1)
    x_step(0)
    x_step(1)
    x_step(2)
    x_step(3)
    hand_on_part(2)
    hand_on_part(3)
    y_step(0)
    y_step(1)
    y_step(2)
    y_step(3)
    layer_out[0] = nn(attn[...], w[...]).astype(BF16)
    z_step(0)
    z_step(1)
    gather_x(0)
    z_step(2)
    gather_x(1)
    z_step(3)
    gather_x(2)
    gather_core(0)
    gather_x(3)
    gather_core(1)
    gather_core(2)
    gather_core(3)

    for p in range(PAIRS):
        for i in range(2):
            for j in range(2):
                part(p, i, j).wait_recv()
    for i, out in enumerate((grad_k, grad_v)):
        out[0] = (own[i] + part_in[i, 0].astype(F32) + part_in[i, 1].astype(F32)).astype(BF16)

    for yi in range(NY):
        remote(gw.at[c, :, yi], gw.at[1 - c, :, yi], gc_s.at[yi], gc_r.at[yi], other).wait_recv()
    for p in range(PAIRS):
        for j in range(2):
            halo(p, 0, j).wait_send()
            part(p, 0, j).wait_send()

        @pl.when(first)
        def _():
            halo(p, 1, 0).wait_send()
            part(p, 1, 1).wait_send()
            to_relay(p, 0).wait_send()

        @pl.when(last)
        def _():
            halo(p, 1, 1).wait_send()
            part(p, 1, 0).wait_send()
            to_relay(p, 1).wait_send()

        @pl.when(jnp.logical_or(second, third))
        def _():
            for j in range(2):
                halo(p, 1, j).wait_send()
                part(p, 1, j).wait_send()
            handed_on(p, 0).wait_send()
            from_relay(p, 0).wait_send()

    for copy in pending:
        copy.wait_send()
    for i in z_away:
        to_z(i).wait_send()
    for i in y_away:
        to_y(i).wait_send()
    for p in range(PAIRS):
        for half in range(2):
            @pl.when(y != 2 * p + half)
            def _():
                remote(
                    y_out.at[p, pl.ds(half * 16, 16)], y_in.at[0],
                    y_s.at[p, half], y_r.at[0], other,
                ).wait_send()


def finish(layer_out_in, grad_q_in, grad_k_in, grad_v_in, gw, layer_out, grad_q, grad_k, grad_v, grad_w, total, sems):
    copies = []
    for src, dst in (
        (layer_out_in, layer_out), (grad_q_in, grad_q), (grad_k_in, grad_k), (grad_v_in, grad_v),
    ):
        copies.append(pltpu.make_async_copy(src, dst, sems.at[len(copies)]))
        copies[-1].start()
    scale = 1.0 / math.sqrt(TOK * NX * NY * NZ * NC)
    for yi in range(NY):
        for ci in range(NC):
            for xi in range(NX):
                row = (yi // 2) * 128 + xi * 32 + (yi % 2) * 16
                total[row:row + 16, ci * 256:ci * 256 + 256] = gw[ci, xi, yi].astype(F32) * scale
        if yi % 2:
            rows = pl.ds(yi // 2 * 128, 128)
            copies.append(pltpu.make_async_copy(total.at[rows], grad_w.at[rows], sems.at[len(copies)]))
            copies[-1].start()
    for copy in copies:
        copy.wait()


def body(query, key, value, table, out_weight, cotangent):
    vmem = pl.BlockSpec(memory_space=pltpu.VMEM)
    dma = pltpu.SemaphoreType.DMA
    like = jax.ShapeDtypeStruct((1, TOK, D), BF16)
    shapes = (like, like, like, like)
    anywhere = pl.BlockSpec(memory_space=pl.ANY)
    raw = pl.pallas_call(
        kernel,
        out_shape=shapes + (jax.ShapeDtypeStruct((NC, NX, NY, 16, 256), BF16),),
        in_specs=[anywhere] * 6,
        out_specs=(vmem,) * 5,
        scratch_shapes=[
            pltpu.SMEM((2, 4), jnp.int32),
            pltpu.VMEM((1, TOK, D), BF16), pltpu.VMEM((D, D), BF16), pltpu.VMEM((1, TOK, D), BF16),
            pltpu.VMEM((WIN, D), BF16), pltpu.VMEM((WIN, D), BF16),
            pltpu.VMEM((TOK, D), BF16), pltpu.VMEM((TOK, D), BF16), pltpu.VMEM((2 * TOK, WIN), F32),
            pltpu.VMEM((2, 2, TOK, D), BF16), pltpu.VMEM((2, 2, TOK, D), BF16), pltpu.VMEM((2, TOK, D), F32),
            pltpu.VMEM((PAIRS, 128, 256), BF16), pltpu.VMEM((PAIRS, 128, 256), BF16), pltpu.VMEM((PAIRS, 128, 256), F32),
            pltpu.VMEM((PAIRS, 128, 256), BF16), pltpu.VMEM((PAIRS, NX - 1, 32, 256), BF16), pltpu.VMEM((PAIRS, 128, 256), F32),
            pltpu.VMEM((PAIRS, 32, 256), BF16), pltpu.VMEM((NY - 1, 16, 256), BF16), pltpu.VMEM((16, 256), F32),
            pltpu.VMEM((NZ, 16, 256), BF16),
            pltpu.VMEM((TOK, D), BF16), dma((6,)), dma((PAIRS, 2, 2)), dma((PAIRS, 2, 2)),
            dma((PAIRS,)), dma((PAIRS,)), dma((PAIRS,)), dma((PAIRS,)),
            dma((PAIRS, 2, 2)), dma((PAIRS, 2, 2)),
            dma((PAIRS,)), dma((PAIRS,)), dma((PAIRS, NX - 1)), dma((PAIRS, NX - 1)),
            dma((PAIRS, 2)), dma((NY - 1,)), dma((NZ - 1,)), dma((NZ,)),
            dma((NY - 1,)), dma((NY,)), dma((NY, NX - 1)), dma((NY, NX)), dma((NY,)), dma((NY,)),
        ],
        compiler_params=pltpu.CompilerParams(collective_id=0, has_side_effects=True),
    )(table, query, key, value, out_weight, cotangent)
    return tuple(pl.pallas_call(
        finish,
        out_shape=shapes + (jax.ShapeDtypeStruct((D, D), F32),),
        in_specs=[vmem] * 5,
        out_specs=(anywhere,) * 5,
        scratch_shapes=[pltpu.VMEM((D, D), F32), dma((8,))],
    )(*raw))


def solution(mesh):
    rows = P("dp", "ctx", None)
    return jax.shard_map(
        body,
        mesh=mesh,
        in_specs=(rows, rows, rows, P("ctx", None), P(), rows),
        out_specs=(rows, rows, rows, rows, P()),
        check_vma=False,
    )
```
